32 devices in a mesh: groups: 2 (over x), owner: 16 (over z, y, core).
Axes of the slice: x: 2, y: 2, z: 4, core: 2. Of those that a mesh axis runs over, the one named last changes fastest.
Arguments:
- tokens: bfloat16 [512, 8192], P(('groups', 'owner')), parts along dimension 0, may hold values from -6 to 6
- base_weight: bfloat16 [2, 8192, 16384], P(None, None, 'owner'), may hold values from -0.0625 to 0.0625
- adapter_down: float32 [32, 32, 8192], P(('groups', 'owner')), parts along dimension 0, may hold values from -0.0625 to 0.0625
- adapter_up: float32 [32, 2, 16, 16384], P(('groups', 'owner')), parts along dimension 0, may hold values from -1.5 to 1.5
- adapter_id: int32 [512, 1], P('groups'), parts along dimension 0, may hold values from 0 to 15; in each aligned block of 256 rows (0 to 255, 256 to 511, ...) at most 32 rows name the same one
- owner_of: int32 [32], P('groups'), parts along dimension 0, may hold values from 0 to 15, each once
Outputs:
- hidden: bfloat16 [512, 16384], P('groups', 'owner'), parts along dimension 0
The draws below stay inside these ranges and needn't reach their ends.
There are 2 independent parts, one for each index of `groups`. The reference program is written for one: setup_inputs(seed, part) draws one part's arguments, and reference() takes and returns one part's arrays. A program takes and returns all parts, laid end to end along the dimension named above; an argument that names none is the same for every part. Nothing has to cross between parts.
Inputs may be any that keep to these rules, and one draw needn't show every extreme that they name: `adapter_id`: no adapter is named by more than 32 rows of a part, a bound that some block reaches. `owner_of`: A permutation: every owner index holds exactly one adapter.
All inputs are finite; a program needn't handle non-finite values.
Results may differ from the reference program's by a relative error of at most 0.0052.
Values may be sent and summed in bfloat16 or wider, within the bound.
A program may use at most 128 MiB of HBM per device.

```python
import math
import jax
import jax.numpy as jnp
import numpy as np
from jax import lax

D = 8192
FF = 16384
LOWRANK = 16
ROWS = 256
ADAPTERS = 16
CAP = 32


def block_scale(rng, extent, pieces, smallest, top_value):
    gain, own = 1.0, jax.random.fold_in(rng, 6)
    for axis_at, shards_of in pieces:
        draws = jnp.exp(jax.random.uniform(jax.random.fold_in(own, axis_at), (shards_of,), jnp.float32, smallest / len(pieces), top_value / len(pieces)))
        gain = gain * jnp.repeat(draws, extent[axis_at] // shards_of).reshape([-1 if axis == axis_at else 1 for axis in range(len(extent))])
    return gain


def routed_block(rng, own, number, rows, number_of, top, bound, skew):
    order = jax.random.permutation(rng, number_of)
    crowded, usual = shares(number_of, rows * top, bound, skew, True), shares(number_of, rows * top, bound, skew, False)
    places = jnp.arange(number_of)

    def named(lengths, turn):
        used = int((lengths > 0).sum())
        fixed = max(1, used // 4)
        shifted = fixed + (places - fixed + turn * (used - fixed)) % max(1, number_of - fixed)
        return jnp.zeros((number_of,), jnp.int32).at[order[jnp.where(places < fixed, places, shifted)]].set(jnp.asarray(lengths, jnp.int32))

    lengths = jnp.where(number % 4 == 0, named(crowded, number // 4), named(usual, number - number // 4 - 1))
    mixed = jax.random.permutation(jax.random.fold_in(own, 3), number_of)
    giver, receiver = mixed[0:number_of // 2 * 2:2], mixed[1:number_of // 2 * 2:2]
    margin = jnp.minimum(lengths[giver] - 1, bound - lengths[receiver]) // 2
    margin = jnp.where((giver == order[0]) | (receiver == order[0]) | (lengths[receiver] == 0), 0, jnp.maximum(margin, 0))
    shifted = jax.random.randint(jax.random.fold_in(own, 4), (number_of // 2,), 0, 1 << 20) % (margin + 1)
    lengths = lengths.at[giver].add(-shifted).at[receiver].add(shifted)
    labels = jnp.searchsorted(jnp.cumsum(lengths), jnp.arange(rows * top), side="right").astype(jnp.int32)
    listing = labels.reshape(top, rows).T
    listing = listing[jax.random.permutation(jax.random.fold_in(own, 1), rows)]
    turn = jax.random.randint(jax.random.fold_in(own, 2), (rows, 1), 0, top)
    return jnp.take_along_axis(listing, (jnp.arange(top)[None, :] + turn) % top, axis=1)


def shares(count, total, limit, lean, full):
    loads = [(1 << 20) // math.isqrt(rank ** lean) + 1 for rank in range(1, count + 1)]
    largest = limit if full else min(limit, max(-(-total // count), total * loads[0] // sum(loads)))
    least = 1 if total - largest >= count - 1 else 0
    holding, rest = [largest] + [least] * (count - 1), total - largest - least * (count - 1)
    while rest > 0:
        movable = [i for i in range(1, count) if holding[i] < largest] or [i for i in range(1, count) if holding[i] < limit]
        pool, budget = sum([loads[i] for i in movable]), rest
        for i in movable:
            more = min(limit - holding[i], max(1, budget * loads[i] // pool), rest)
            holding[i] = holding[i] + more
            rest = rest - more
    return np.array(holding)


def gaussian(rng, extent, width, most, split=(), kind=jnp.bfloat16):
    array = jax.random.normal(rng, extent, jnp.float32) * width
    if len(split) > 0:
        array = block_scale(rng, extent, split, -0.22, 0.18) * array
    return jnp.clip(array, min=-most, max=most).astype(kind)


def setup_inputs(seed: int = 0, part: int = 0) -> dict:
    streams_of = jax.random.split(jax.random.key(seed), 7)
    part_keys = jax.random.split(jax.random.fold_in(streams_of[6], part), 7)
    tokens = gaussian(part_keys[0], (ROWS, D), 1.0, 6.0, ((0, 16),))
    base_weight = gaussian(streams_of[1], (2, D, FF), D ** -0.5, 0.0625, ((2, 16),))
    adapter_down = gaussian(part_keys[2], (ADAPTERS, 2 * LOWRANK, D), D ** -0.5, 0.0625, ((0, 16),), jnp.float32)
    adapter_up = gaussian(part_keys[3], (ADAPTERS, 2, LOWRANK, FF), 0.25, 1.5, ((0, 16),), jnp.float32)
    adapter_id_keys = jax.random.split(jax.random.fold_in(part_keys[4], 1), ROWS // ROWS)
    adapter_id_turns = jax.random.permutation(jax.random.fold_in(part_keys[4], 3), ROWS // ROWS)
    adapter_id = jax.vmap(lambda own, number: routed_block(jax.random.fold_in(part_keys[4], 2), own, number, ROWS, ADAPTERS, 1, CAP, 2))(adapter_id_keys, adapter_id_turns).reshape((ROWS, 1))
    owner_of = jax.random.permutation(part_keys[5], ADAPTERS).astype(jnp.int32)
    return dict(tokens=tokens, base_weight=base_weight, adapter_down=adapter_down, adapter_up=adapter_up, adapter_id=adapter_id, owner_of=owner_of)


def reference(tokens, base_weight, adapter_down, adapter_up, adapter_id, owner_of):
    home = owner_of[adapter_id[:, 0]].astype(jnp.int32)

    def per_row(packed):
        token_row, owner_row = packed
        factor_one = adapter_down[owner_row]
        codes_row = jnp.dot(factor_one, token_row.astype(jnp.float32), precision=lax.Precision.HIGHEST)
        factor_two = adapter_up[owner_row]
        term_row = jnp.einsum("pk,pkf->pf", codes_row.reshape(2, LOWRANK), factor_two, precision=lax.Precision.HIGHEST)
        return term_row.astype(jnp.bfloat16)

    term = lax.map(per_row, (tokens, home)).astype(jnp.float32)
    gate_base = jnp.dot(tokens, base_weight[0], preferred_element_type=jnp.float32)
    up_base = jnp.dot(tokens, base_weight[1], preferred_element_type=jnp.float32)
    gate_pre = gate_base + term[:, 0, :]
    up_pre = up_base + term[:, 1, :]
    hidden = jax.nn.silu(gate_pre) * up_pre
    return hidden.astype(jnp.bfloat16)
```

```python
import functools

import jax
import jax.numpy as jnp
from jax import lax
from jax.experimental import pallas as pl
from jax.experimental.pallas import tpu as pltpu
from jax.sharding import PartitionSpec as P

CAP = 32
CHUNKS = 4
COLUMN_TILE = 256
HIGHEST = lax.Precision.HIGHEST


def on_device(tokens, base_weight, adapter_down, adapter_up, adapter_id, owner_of):
    owners = lax.axis_size("owner")
    own_index = lax.axis_index("owner")
    rows_dev = tokens.shape[0]
    row_count = rows_dev * owners
    ff_dev = base_weight.shape[2]
    lowrank = adapter_up.shape[2]
    table_hits = (adapter_id[:, 0][:, None] == jnp.arange(owners, dtype=jnp.int32)[None, :]).astype(
        jnp.int32
    )
    home = jnp.sum(table_hits * owner_of[None, :], axis=1)
    member = (home[:, None] == jnp.arange(owners, dtype=jnp.int32)[None, :]).astype(jnp.int32)
    before = jnp.cumsum(member, axis=0) - member
    bucket_slot = jnp.sum(before * member, axis=1)
    mine = (home == own_index).astype(jnp.int32)
    matched = (bucket_slot[None, :] == jnp.arange(CAP, dtype=jnp.int32)[:, None]).astype(
        jnp.int32
    ) * mine[None, :]
    bucket_row = jnp.sum(matched * jnp.arange(row_count, dtype=jnp.int32)[None, :], axis=1)
    filled = jnp.sum(matched, axis=1)
    piece = lax.all_gather(tokens, "owner", axis=0, tiled=True)
    gate_out = jnp.dot(piece, base_weight[0], preferred_element_type=jnp.float32)
    up_out = jnp.dot(piece, base_weight[1], preferred_element_type=jnp.float32)
    fetched = jnp.take(piece, jnp.clip(bucket_row, 0, row_count - 1), axis=0)
    picked = jnp.where((filled > 0)[:, None], fetched.astype(jnp.float32), 0.0)
    codes = lax.dot_general(picked, adapter_down[0], (((1,), (1,)), ((), ())), precision=HIGHEST)
    factor_local = adapter_up[0].reshape(2, lowrank, owners, ff_dev)
    full_terms = jnp.einsum(
        "cpk,pkof->cpof",
        codes.reshape(CAP, 2, lowrank),
        factor_local,
        precision=HIGHEST,
    )
    full_terms = full_terms.astype(jnp.bfloat16)
    received = lax.all_to_all(full_terms, "owner", split_axis=2, concat_axis=2, tiled=True)
    adapter_term = received[bucket_slot, :, home, :].astype(jnp.float32)
    hidden = jax.nn.silu(gate_out + adapter_term[:, 0, :]) * (up_out + adapter_term[:, 1, :])
    return hidden.astype(jnp.bfloat16)


def split_two(value):
    high = value.astype(jnp.bfloat16)
    low = (value - high.astype(jnp.float32)).astype(jnp.bfloat16)
    return high, low


def iota(shape, dim):
    return lax.broadcasted_iota(jnp.int32, shape, dim)


def kernel(
    depth_z,
    width_y,
    id_ref,
    owner_ref,
    tok_hbm,
    w_hbm,
    down_hbm,
    up_hbm,
    out_ref,
    gathered,
    weights,
    down,
    up_wide,
    up_send,
    up_all,
    packed,
    total,
    code_total,
    local_sem,
    weight_sem,
    token_sem,
    send_sem,
    recv_sem,
    factor_send,
    factor_recv,
    code_send,
    code_recv,
):
    n = depth_z * width_y * 2
    chunks = gathered.shape[0]
    rows_dev = gathered.shape[2]
    wide = gathered.shape[3]
    rows = n * rows_dev
    ff = weights.shape[2]
    rank = up_all.shape[2]
    me = lax.axis_index("owner")
    core = lax.rem(me, 2)
    y = lax.rem(me // 2, width_y)
    z = me // (2 * width_y)

    def index(zz, yy, cc):
        return (zz * width_y + yy) * 2 + cc

    def peer(j):
        return lax.rem(me + j, n)

    def token_copy(c):
        return pltpu.make_async_copy(
            tok_hbm.at[:, pl.ds(c * wide, wide)], gathered.at[c, me], token_sem.at[c]
        )

    for c in range(chunks):
        token_copy(c).start()
    up_copy = pltpu.make_async_copy(up_hbm.at[0], up_wide, local_sem.at[0])
    up_copy.start()

    def weight_copy(c):
        part = pl.ds(pl.multiple_of(c * wide, wide), wide)
        return pltpu.make_async_copy(w_hbm.at[:, part], weights.at[:, part], weight_sem.at[c])

    for c in range(chunks):
        weight_copy(c).start()
    down_copy = pltpu.make_async_copy(down_hbm.at[0], down, local_sem.at[1])
    down_copy.start()

    barrier = pltpu.get_barrier_semaphore()
    for j in range(1, n):
        pl.semaphore_signal(
            barrier, inc=1, device_id={"owner": peer(j)}, device_id_type=pl.DeviceIdType.MESH
        )
    pl.semaphore_wait(barrier, n - 1)

    def block_copy(kind, c, o, target):
        return pltpu.make_async_remote_copy(
            src_ref=gathered.at[c, o],
            dst_ref=gathered.at[c, o],
            send_sem=send_sem.at[kind, c, o],
            recv_sem=recv_sem.at[c, o],
            device_id={"owner": target},
            device_id_type=pl.DeviceIdType.MESH,
        )

    def upward(c, o):
        return block_copy(0, c, o, index(lax.rem(z + 1, depth_z), y, core))

    def downward(c, o):
        return block_copy(1, c, o, index(lax.rem(z + depth_z - 1, depth_z), y, core))

    def across(c, o):
        return block_copy(2, c, o, index(z, 1 - y, core))

    def sibling(c, o):
        return block_copy(3, c, o, index(z, y, 1 - core))

    def own_sends(c):
        token_copy(c).wait()

        @pl.when(z < depth_z - 1)
        def _():
            upward(c, me).start()

        @pl.when(z > 0)
        def _():
            downward(c, me).start()

        if width_y > 1:
            across(c, me).start()
        sibling(c, me).start()

    def factor_copy(j):
        return pltpu.make_async_remote_copy(
            src_ref=up_send.at[peer(j)],
            dst_ref=up_all.at[:, me],
            send_sem=factor_send.at[j],
            recv_sem=factor_recv.at[j],
            device_id={"owner": peer(j)},
            device_id_type=pl.DeviceIdType.MESH,
        )

    def code_copy(j):
        return pltpu.make_async_remote_copy(
            src_ref=packed.at[me],
            dst_ref=packed.at[me],
            send_sem=code_send.at[j],
            recv_sem=code_recv.at[j],
            device_id={"owner": peer(j)},
            device_id_type=pl.DeviceIdType.MESH,
        )

    own_sends(0)
    up_copy.wait()
    for o in range(n):
        up_send[o] = up_wide[:, :, o * ff : (o + 1) * ff].astype(jnp.bfloat16)
    up_all[:, pl.ds(me, 1)] = up_send[pl.ds(me, 1)].reshape(2, 1, rank, ff)

    def relay(c):
        for d in range(1, depth_z):

            @pl.when(z >= d)
            def _():
                o = index(z - d, y, core)
                upward(c, o).wait_recv()

                @pl.when(z < depth_z - 1)
                def _():
                    upward(c, o).start()

                if width_y > 1:
                    across(c, o).start()
                sibling(c, o).start()

            @pl.when(z + d < depth_z)
            def _():
                o = index(z + d, y, core)
                downward(c, o).wait_recv()

                @pl.when(z > 0)
                def _():
                    downward(c, o).start()

                if width_y > 1:
                    across(c, o).start()
                sibling(c, o).start()

        if width_y > 1:
            for d in range(depth_z):
                o = index(lax.rem(z + d, depth_z), 1 - y, core)
                across(c, o).wait_recv()
                sibling(c, o).start()
        for zz in range(depth_z):
            for yy in range(width_y):
                sibling(c, index(zz, yy, 1 - core)).wait_recv()

    total[...] = jnp.zeros_like(total)
    code_total[...] = jnp.zeros_like(code_total)
    down_copy.wait()

    def multiply(c):
        part = pl.ds(pl.multiple_of(c * wide, wide), wide)
        weight_copy(c).wait()
        high, low = split_two(down[:, part])
        factors = jnp.concatenate([high] * 4 + [low] * 4, axis=0)
        code_total[...] += lax.dot_general(
            gathered[c].reshape(rows, wide),
            factors,
            (((1,), (1,)), ((), ())),
            preferred_element_type=jnp.float32,
        )
        for p in range(2):

            @pl.loop(0, ff // COLUMN_TILE)
            def _(t):
                columns = pl.ds(pl.multiple_of(t * COLUMN_TILE, COLUMN_TILE), COLUMN_TILE)
                total[p, :, columns] += jnp.dot(
                    gathered[c].reshape(rows, wide),
                    weights[p, part, columns],
                    preferred_element_type=jnp.float32,
                )

    per_step = -(-(n - 1) // chunks)
    for c in range(chunks):
        if c + 1 < chunks:
            own_sends(c + 1)
        for j in range(1 + c * per_step, min(n, 1 + (c + 1) * per_step)):
            factor_copy(j).start()
        relay(c)
        multiply(c)

    ids = id_ref[...]
    hit = ids == iota((rows, n), 1)
    home = jnp.sum(jnp.where(hit, owner_ref[...], 0).astype(jnp.float32), axis=1, keepdims=True)
    home = home.astype(jnp.int32)
    member = (home == iota((rows, 128), 1)).astype(jnp.float32)
    lower = (iota((rows, rows), 1) < iota((rows, rows), 0)).astype(jnp.bfloat16)
    before = jnp.dot(lower, member.astype(jnp.bfloat16), preferred_element_type=jnp.float32)
    slot = jnp.sum(before * member, axis=1, keepdims=True).astype(jnp.int32)
    slot_low, slot_high = lax.rem(slot, 8), slot // 8
    lane_group = iota((rows, 128), 1) // (2 * rank)
    codes = code_total[:, :128] + code_total[:, 128:]
    placed = jnp.where((lane_group == slot_high) & (home == me), codes, 0.0)
    pick = (slot_low == iota((rows, 8), 1)).astype(jnp.float32)
    packed[me] = lax.dot_general(
        pick, placed, (((0,), (0,)), ((), ())), precision=HIGHEST, preferred_element_type=jnp.float32
    )
    for j in range(1, n):
        code_copy(j).start()
    back = (home * 8 + slot_low == iota((rows, n * 8), 1)).astype(jnp.float32)
    for j in range(1, n):
        code_copy(j).wait()
    rows_codes = jnp.dot(
        back, packed[...].reshape(n * 8, 128), precision=HIGHEST, preferred_element_type=jnp.float32
    )
    rows_codes = jnp.where(lane_group == slot_high, rows_codes, 0.0)
    spread = []
    for p in range(2):
        place = lax.rem(iota((128, n * rank), 0), 2 * rank)
        place = place == p * rank + lax.rem(iota((128, n * rank), 1), rank)
        value = jnp.dot(
            rows_codes, place.astype(jnp.float32), precision=HIGHEST, preferred_element_type=jnp.float32
        )
        spread.append(split_two(jnp.where(iota((rows, n * rank), 1) // rank == home, value, 0.0)))

    for j in range(1, n):
        factor_copy(j).wait()

    def preact(p, lo, hi):
        factors = up_all[p].reshape(n * rank, ff)[:, lo:hi]
        term = jnp.dot(spread[p][0], factors, preferred_element_type=jnp.float32)
        term += jnp.dot(spread[p][1], factors, preferred_element_type=jnp.float32)
        return total[p, :, lo:hi] + term.astype(jnp.bfloat16).astype(jnp.float32)

    for lo in range(0, ff, COLUMN_TILE):
        gate = preact(0, lo, lo + COLUMN_TILE)
        up = preact(1, lo, lo + COLUMN_TILE)
        out_ref[:, lo : lo + COLUMN_TILE] = (gate / (1.0 + jnp.exp(-gate)) * up).astype(out_ref.dtype)

    for c in range(chunks):
        for zz in range(depth_z):
            o = index(zz, y, core)

            @pl.when((z < depth_z - 1) & (zz <= z))
            def _():
                upward(c, o).wait_send()

            @pl.when((z > 0) & (zz >= z))
            def _():
                downward(c, o).wait_send()

            if width_y > 1:
                across(c, o).wait_send()
            for yy in range(width_y):
                sibling(c, index(zz, yy, core)).wait_send()


def fused(depth_z, width_y, tokens, base_weight, adapter_down, adapter_up, adapter_id, owner_of):
    n = depth_z * width_y * 2
    rows_dev, d = tokens.shape
    ff = base_weight.shape[2]
    rank = adapter_up.shape[2]
    rows = rows_dev * n
    wide = d // CHUNKS
    any_space = pl.BlockSpec(memory_space=pl.ANY)
    vmem = pl.BlockSpec(memory_space=pltpu.VMEM)
    dma = pltpu.SemaphoreType.DMA
    return pl.pallas_call(
        functools.partial(kernel, depth_z, width_y),
        out_shape=jax.ShapeDtypeStruct((rows, ff), jnp.bfloat16),
        in_specs=[vmem, vmem, any_space, any_space, any_space, any_space],
        out_specs=vmem,
        scratch_shapes=[
            pltpu.VMEM((CHUNKS, n, rows_dev, wide), jnp.bfloat16),
            pltpu.VMEM((2, d, ff), jnp.bfloat16),
            pltpu.VMEM((2 * rank, d), jnp.float32),
            pltpu.VMEM((2, rank, n * ff), jnp.float32),
            pltpu.VMEM((n, 2, rank, ff), jnp.bfloat16),
            pltpu.VMEM((2, n, rank, ff), jnp.bfloat16),
            pltpu.VMEM((n, 8, 128), jnp.float32),
            pltpu.VMEM((2, rows, ff), jnp.float32),
            pltpu.VMEM((rows, 256), jnp.float32),
            dma((2,)),
            dma((CHUNKS,)),
            dma((CHUNKS,)),
            dma((4, CHUNKS, n)),
            dma((CHUNKS, n)),
            dma((n,)),
            dma((n,)),
            dma((n,)),
            dma((n,)),
        ],
        compiler_params=pltpu.CompilerParams(
            collective_id=0, has_side_effects=True, vmem_limit_bytes=60 * 1024 * 1024
        ),
        cost_estimate=pl.CostEstimate(
            flops=4 * rows * d * ff, bytes_accessed=4 * d * ff, transcendentals=rows * ff
        ),
    )(adapter_id, owner_of.reshape(1, n), tokens, base_weight, adapter_down, adapter_up)


def solution(mesh):
    owners = mesh.shape["owner"]
    width_y = 4 // mesh.shape["groups"]
    depth_z = owners // (2 * width_y)
    plan = functools.partial(fused, depth_z, width_y) if owners <= 16 else on_device
    return jax.shard_map(
        plan,
        mesh=mesh,
        in_specs=(
            P(("groups", "owner"), None),
            P(None, None, "owner"),
            P(("groups", "owner"), None, None),
            P(("groups", "owner"), None, None, None),
            P("groups", None),
            P("groups"),
        ),
        out_specs=P("groups", "owner"),
        check_vma=False,
    )
```

```python
import functools

import jax
import jax.numpy as jnp
from jax import lax
from jax.experimental import pallas as pl
from jax.experimental.pallas import tpu as pltpu
from jax.sharding import PartitionSpec as P

CAP = 32
CHUNKS = 4
COLUMN_TILE = 512
FACTORS_PER_TICK = 15
FACTOR_TICK = 4
HIGHEST = lax.Precision.HIGHEST


def on_device(tokens, base_weight, adapter_down, adapter_up, adapter_id, owner_of):
    owners = lax.axis_size("owner")
    own_index = lax.axis_index("owner")
    rows_dev = tokens.shape[0]
    row_count = rows_dev * owners
    ff_dev = base_weight.shape[2]
    lowrank = adapter_up.shape[2]
    table_hits = (adapter_id[:, 0][:, None] == jnp.arange(owners, dtype=jnp.int32)[None, :]).astype(
        jnp.int32
    )
    home = jnp.sum(table_hits * owner_of[None, :], axis=1)
    member = (home[:, None] == jnp.arange(owners, dtype=jnp.int32)[None, :]).astype(jnp.int32)
    before = jnp.cumsum(member, axis=0) - member
    bucket_slot = jnp.sum(before * member, axis=1)
    mine = (home == own_index).astype(jnp.int32)
    matched = (bucket_slot[None, :] == jnp.arange(CAP, dtype=jnp.int32)[:, None]).astype(
        jnp.int32
    ) * mine[None, :]
    bucket_row = jnp.sum(matched * jnp.arange(row_count, dtype=jnp.int32)[None, :], axis=1)
    filled = jnp.sum(matched, axis=1)
    piece = lax.all_gather(tokens, "owner", axis=0, tiled=True)
    gate_out = jnp.dot(piece, base_weight[0], preferred_element_type=jnp.float32)
    up_out = jnp.dot(piece, base_weight[1], preferred_element_type=jnp.float32)
    fetched = jnp.take(piece, jnp.clip(bucket_row, 0, row_count - 1), axis=0)
    picked = jnp.where((filled > 0)[:, None], fetched.astype(jnp.float32), 0.0)
    codes = lax.dot_general(picked, adapter_down[0], (((1,), (1,)), ((), ())), precision=HIGHEST)
    factor_local = adapter_up[0].reshape(2, lowrank, owners, ff_dev)
    full_terms = jnp.einsum(
        "cpk,pkof->cpof",
        codes.reshape(CAP, 2, lowrank),
        factor_local,
        precision=HIGHEST,
    )
    full_terms = full_terms.astype(jnp.bfloat16)
    received = lax.all_to_all(full_terms, "owner", split_axis=2, concat_axis=2, tiled=True)
    adapter_term = received[bucket_slot, :, home, :].astype(jnp.float32)
    hidden = jax.nn.silu(gate_out + adapter_term[:, 0, :]) * (up_out + adapter_term[:, 1, :])
    return hidden.astype(jnp.bfloat16)


def split_two(value):
    high = value.astype(jnp.bfloat16)
    low = (value - high.astype(jnp.float32)).astype(jnp.bfloat16)
    return high, low


def iota(shape, dim):
    return lax.broadcasted_iota(jnp.int32, shape, dim)


def kernel(
    depth_z,
    width_y,
    id_ref,
    owner_ref,
    tok_hbm,
    w_hbm,
    down_hbm,
    up_hbm,
    out_ref,
    gathered,
    weights,
    down,
    up_wide,
    up_send,
    up_all,
    packed,
    total,
    code_total,
    local_sem,
    weight_sem,
    token_sem,
    send_sem,
    recv_sem,
    factor_send,
    factor_recv,
    code_send,
    code_recv,
):
    n = depth_z * width_y * 2
    chunks = gathered.shape[0]
    rows_dev = gathered.shape[2]
    wide = gathered.shape[3]
    rows = n * rows_dev
    ff = weights.shape[2]
    rank = up_all.shape[2]
    me = lax.axis_index("owner")
    core = lax.rem(me, 2)
    y = lax.rem(me // 2, width_y)
    z = me // (2 * width_y)

    def index(zz, yy, cc):
        return (zz * width_y + yy) * 2 + cc

    def peer(j):
        return lax.rem(me + j, n)

    def token_copy(c):
        return pltpu.make_async_copy(
            tok_hbm.at[:, pl.ds(c * wide, wide)], gathered.at[c, me], token_sem.at[c]
        )

    for c in range(chunks):
        token_copy(c).start()
    up_copy = pltpu.make_async_copy(up_hbm.at[0], up_wide, local_sem.at[0])
    up_copy.start()

    def weight_copy(c):
        part = pl.ds(pl.multiple_of(c * wide, wide), wide)
        return pltpu.make_async_copy(w_hbm.at[:, part], weights.at[:, part], weight_sem.at[c])

    for c in range(chunks):
        weight_copy(c).start()
    down_copy = pltpu.make_async_copy(down_hbm.at[0], down, local_sem.at[1])
    down_copy.start()

    barrier = pltpu.get_barrier_semaphore()
    for j in range(1, n):
        pl.semaphore_signal(
            barrier, inc=1, device_id={"owner": peer(j)}, device_id_type=pl.DeviceIdType.MESH
        )
    pl.semaphore_wait(barrier, n - 1)

    def block_copy(kind, c, o, target):
        return pltpu.make_async_remote_copy(
            src_ref=gathered.at[c, o],
            dst_ref=gathered.at[c, o],
            send_sem=send_sem.at[kind, c, o],
            recv_sem=recv_sem.at[c, o],
            device_id={"owner": target},
            device_id_type=pl.DeviceIdType.MESH,
        )

    def upward(c, o):
        return block_copy(0, c, o, index(lax.rem(z + 1, depth_z), y, core))

    def downward(c, o):
        return block_copy(1, c, o, index(lax.rem(z + depth_z - 1, depth_z), y, core))

    def across(c, o):
        return block_copy(2, c, o, index(z, 1 - y, core))

    def sibling(c, o):
        return block_copy(3, c, o, index(z, y, 1 - core))

    def own_sends(c):
        token_copy(c).wait()

        @pl.when(z < depth_z - 1)
        def _():
            upward(c, me).start()

        @pl.when(z > 0)
        def _():
            downward(c, me).start()

        if width_y > 1:
            across(c, me).start()
        sibling(c, me).start()

    def factor_copy(j):
        return pltpu.make_async_remote_copy(
            src_ref=up_send.at[peer(j)],
            dst_ref=up_all.at[:, me],
            send_sem=factor_send.at[j],
            recv_sem=factor_recv.at[j],
            device_id={"owner": peer(j)},
            device_id_type=pl.DeviceIdType.MESH,
        )

    def code_copy(j):
        return pltpu.make_async_remote_copy(
            src_ref=packed.at[me],
            dst_ref=packed.at[me],
            send_sem=code_send.at[j],
            recv_sem=code_recv.at[j],
            device_id={"owner": peer(j)},
            device_id_type=pl.DeviceIdType.MESH,
        )

    for c in range(chunks):
        own_sends(c)
    up_copy.wait()
    for o in range(n):
        up_send[o] = up_wide[:, :, o * ff : (o + 1) * ff].astype(jnp.bfloat16)
    up_all[:, pl.ds(me, 1)] = up_send[pl.ds(me, 1)].reshape(2, 1, rank, ff)

    def hop(c, d):
        for side, arrive, last in ((-1, upward, depth_z - 1), (1, downward, 0)):

            @pl.when((z >= d) if side < 0 else (z + d < depth_z))
            def _():
                o = index(z + side * d, y, core)
                arrive(c, o).wait_recv()

                @pl.when(z != last)
                def _():
                    arrive(c, o).start()

                if width_y > 1:
                    across(c, o).start()
                sibling(c, o).start()

    def land(c, d):
        for zz, there in ((z - d, z >= d), (z + d, z + d < depth_z)):
            there = there if d > 0 else z >= 0

            @pl.when(there)
            def _():
                o = index(zz, 1 - y, core)
                across(c, o).wait_recv()
                sibling(c, o).start()

            if d == 0:
                break

    def complete(c):
        for zz in range(depth_z):
            for yy in range(width_y):
                sibling(c, index(zz, yy, 1 - core)).wait_recv()

    total[...] = jnp.zeros_like(total)
    code_total[...] = jnp.zeros_like(code_total)
    down_copy.wait()

    def code_dot(c):
        part = pl.ds(pl.multiple_of(c * wide, wide), wide)
        high, low = split_two(down[:, part])
        factors = jnp.concatenate([high] * 4 + [low] * 4, axis=0)
        code_total[...] += lax.dot_general(
            gathered[c].reshape(rows, wide),
            factors,
            (((1,), (1,)), ((), ())),
            preferred_element_type=jnp.float32,
        )

    def multiply(c):
        part = pl.ds(pl.multiple_of(c * wide, wide), wide)
        weight_copy(c).wait()
        for p in range(2):

            @pl.loop(0, ff // COLUMN_TILE)
            def _(t):
                columns = pl.ds(pl.multiple_of(t * COLUMN_TILE, COLUMN_TILE), COLUMN_TILE)
                total[p, :, columns] += jnp.dot(
                    gathered[c].reshape(rows, wide),
                    weights[p, part, columns],
                    preferred_element_type=jnp.float32,
                )

    ids = id_ref[...]
    hit = ids == iota((rows, n), 1)
    home = jnp.sum(jnp.where(hit, owner_ref[...], 0).astype(jnp.float32), axis=1, keepdims=True)
    home = home.astype(jnp.int32)
    member = (home == iota((rows, 128), 1)).astype(jnp.float32)
    lower = (iota((rows, rows), 1) < iota((rows, rows), 0)).astype(jnp.bfloat16)
    before = jnp.dot(lower, member.astype(jnp.bfloat16), preferred_element_type=jnp.float32)
    slot = jnp.sum(before * member, axis=1, keepdims=True).astype(jnp.int32)
    slot_low, slot_high = lax.rem(slot, 8), slot // 8
    lane_group = iota((rows, 128), 1) // (2 * rank)
    pick = (slot_low == iota((rows, 8), 1)).astype(jnp.float32)
    back = (home * 8 + slot_low == iota((rows, n * 8), 1)).astype(jnp.float32)

    def share_codes():
        codes = code_total[:, :128] + code_total[:, 128:]
        placed = jnp.where((lane_group == slot_high) & (home == me), codes, 0.0)
        packed[me] = lax.dot_general(
            pick, placed, (((0,), (0,)), ((), ())), precision=HIGHEST, preferred_element_type=jnp.float32
        )
        for j in range(1, n):
            code_copy(j).start()

    def factors_of(tick):
        first = 1 + max(0, tick - FACTOR_TICK) * FACTORS_PER_TICK
        count = FACTORS_PER_TICK if tick >= FACTOR_TICK else 0
        return range(first, n if tick == chunks + depth_z - 1 else min(n, first + count))

    for tick in range(chunks + depth_z):
        for d in range(1, depth_z):
            if 0 <= tick - d + 1 < chunks:
                hop(tick - d + 1, d)
        if width_y > 1:
            for d in range(depth_z):
                if 0 <= tick - d < chunks:
                    land(tick - d, d)
        for j in factors_of(tick):
            factor_copy(j).start()
        if tick >= depth_z:
            complete(tick - depth_z)
            code_dot(tick - depth_z)
            if tick == chunks + depth_z - 1:
                share_codes()
            multiply(tick - depth_z)

    for j in range(1, n):
        code_copy(j).wait()
    rows_codes = jnp.dot(
        back, packed[...].reshape(n * 8, 128), precision=HIGHEST, preferred_element_type=jnp.float32
    )
    rows_codes = jnp.where(lane_group == slot_high, rows_codes, 0.0)
    spread = []
    for p in range(2):
        place = lax.rem(iota((128, n * rank), 0), 2 * rank)
        place = place == p * rank + lax.rem(iota((128, n * rank), 1), rank)
        value = jnp.dot(
            rows_codes, place.astype(jnp.float32), precision=HIGHEST, preferred_element_type=jnp.float32
        )
        spread.append(split_two(jnp.where(iota((rows, n * rank), 1) // rank == home, value, 0.0)))

    for j in range(1, n):
        factor_copy(j).wait()

    def preact(p, lo, hi):
        factors = up_all[p].reshape(n * rank, ff)[:, lo:hi]
        term = jnp.dot(spread[p][0], factors, preferred_element_type=jnp.float32)
        term += jnp.dot(spread[p][1], factors, preferred_element_type=jnp.float32)
        return total[p, :, lo:hi] + term.astype(jnp.bfloat16).astype(jnp.float32)

    for lo in range(0, ff, COLUMN_TILE):
        gate = preact(0, lo, lo + COLUMN_TILE)
        up = preact(1, lo, lo + COLUMN_TILE)
        out_ref[:, lo : lo + COLUMN_TILE] = (gate / (1.0 + jnp.exp(-gate)) * up).astype(out_ref.dtype)

    for c in range(chunks):
        for zz in range(depth_z):
            o = index(zz, y, core)

            @pl.when((z < depth_z - 1) & (zz <= z))
            def _():
                upward(c, o).wait_send()

            @pl.when((z > 0) & (zz >= z))
            def _():
                downward(c, o).wait_send()

            if width_y > 1:
                across(c, o).wait_send()
            for yy in range(width_y):
                sibling(c, index(zz, yy, core)).wait_send()


def fused(depth_z, width_y, tokens, base_weight, adapter_down, adapter_up, adapter_id, owner_of):
    n = depth_z * width_y * 2
    rows_dev, d = tokens.shape
    ff = base_weight.shape[2]
    rank = adapter_up.shape[2]
    rows = rows_dev * n
    wide = d // CHUNKS
    any_space = pl.BlockSpec(memory_space=pl.ANY)
    vmem = pl.BlockSpec(memory_space=pltpu.VMEM)
    dma = pltpu.SemaphoreType.DMA
    return pl.pallas_call(
        functools.partial(kernel, depth_z, width_y),
        out_shape=jax.ShapeDtypeStruct((rows, ff), jnp.bfloat16),
        in_specs=[vmem, vmem, any_space, any_space, any_space, any_space],
        out_specs=vmem,
        scratch_shapes=[
            pltpu.VMEM((CHUNKS, n, rows_dev, wide), jnp.bfloat16),
            pltpu.VMEM((2, d, ff), jnp.bfloat16),
            pltpu.VMEM((2 * rank, d), jnp.float32),
            pltpu.VMEM((2, rank, n * ff), jnp.float32),
            pltpu.VMEM((n, 2, rank, ff), jnp.bfloat16),
            pltpu.VMEM((2, n, rank, ff), jnp.bfloat16),
            pltpu.VMEM((n, 8, 128), jnp.float32),
            pltpu.VMEM((2, rows, ff), jnp.float32),
            pltpu.VMEM((rows, 256), jnp.float32),
            dma((2,)),
            dma((CHUNKS,)),
            dma((CHUNKS,)),
            dma((4, CHUNKS, n)),
            dma((CHUNKS, n)),
            dma((n,)),
            dma((n,)),
            dma((n,)),
            dma((n,)),
        ],
        compiler_params=pltpu.CompilerParams(
            collective_id=0, has_side_effects=True, vmem_limit_bytes=60 * 1024 * 1024
        ),
        cost_estimate=pl.CostEstimate(
            flops=4 * rows * d * ff, bytes_accessed=4 * d * ff, transcendentals=rows * ff
        ),
    )(adapter_id, owner_of.reshape(1, n), tokens, base_weight, adapter_down, adapter_up)


def solution(mesh):
    owners = mesh.shape["owner"]
    width_y = 4 // mesh.shape["groups"]
    depth_z = owners // (2 * width_y)
    plan = functools.partial(fused, depth_z, width_y) if owners <= 16 else on_device
    return jax.shard_map(
        plan,
        mesh=mesh,
        in_specs=(
            P(("groups", "owner"), None),
            P(None, None, "owner"),
            P(("groups", "owner"), None, None),
            P(("groups", "owner"), None, None, None),
            P("groups", None),
            P("groups"),
        ),
        out_specs=P("groups", "owner"),
        check_vma=False,
    )
```

```python
import functools

import jax
import jax.numpy as jnp
from jax import lax
from jax.experimental import pallas as pl
from jax.experimental.pallas import tpu as pltpu
from jax.sharding import PartitionSpec as P

CAP = 32
CHUNKS = 2
COLUMN_TILE = 512
FACTORS_PER_TICK = 15
FACTOR_TICK = 2
HIGHEST = lax.Precision.HIGHEST


def on_device(tokens, base_weight, adapter_down, adapter_up, adapter_id, owner_of):
    owners = lax.axis_size("owner")
    own_index = lax.axis_index("owner")
    rows_dev = tokens.shape[0]
    row_count = rows_dev * owners
    ff_dev = base_weight.shape[2]
    lowrank = adapter_up.shape[2]
    table_hits = (adapter_id[:, 0][:, None] == jnp.arange(owners, dtype=jnp.int32)[None, :]).astype(
        jnp.int32
    )
    home = jnp.sum(table_hits * owner_of[None, :], axis=1)
    member = (home[:, None] == jnp.arange(owners, dtype=jnp.int32)[None, :]).astype(jnp.int32)
    before = jnp.cumsum(member, axis=0) - member
    bucket_slot = jnp.sum(before * member, axis=1)
    mine = (home == own_index).astype(jnp.int32)
    matched = (bucket_slot[None, :] == jnp.arange(CAP, dtype=jnp.int32)[:, None]).astype(
        jnp.int32
    ) * mine[None, :]
    bucket_row = jnp.sum(matched * jnp.arange(row_count, dtype=jnp.int32)[None, :], axis=1)
    filled = jnp.sum(matched, axis=1)
    piece = lax.all_gather(tokens, "owner", axis=0, tiled=True)
    gate_out = jnp.dot(piece, base_weight[0], preferred_element_type=jnp.float32)
    up_out = jnp.dot(piece, base_weight[1], preferred_element_type=jnp.float32)
    fetched = jnp.take(piece, jnp.clip(bucket_row, 0, row_count - 1), axis=0)
    picked = jnp.where((filled > 0)[:, None], fetched.astype(jnp.float32), 0.0)
    codes = lax.dot_general(picked, adapter_down[0], (((1,), (1,)), ((), ())), precision=HIGHEST)
    factor_local = adapter_up[0].reshape(2, lowrank, owners, ff_dev)
    full_terms = jnp.einsum(
        "cpk,pkof->cpof",
        codes.reshape(CAP, 2, lowrank),
        factor_local,
        precision=HIGHEST,
    )
    full_terms = full_terms.astype(jnp.bfloat16)
    received = lax.all_to_all(full_terms, "owner", split_axis=2, concat_axis=2, tiled=True)
    adapter_term = received[bucket_slot, :, home, :].astype(jnp.float32)
    hidden = jax.nn.silu(gate_out + adapter_term[:, 0, :]) * (up_out + adapter_term[:, 1, :])
    return hidden.astype(jnp.bfloat16)


def split_two(value):
    high = value.astype(jnp.bfloat16)
    low = (value - high.astype(jnp.float32)).astype(jnp.bfloat16)
    return high, low


def iota(shape, dim):
    return lax.broadcasted_iota(jnp.int32, shape, dim)


def kernel(
    depth_z,
    width_y,
    id_ref,
    owner_ref,
    tok_hbm,
    w_hbm,
    down_hbm,
    up_hbm,
    out_ref,
    gathered,
    weights,
    down,
    up_wide,
    up_send,
    up_all,
    packed,
    total,
    code_total,
    local_sem,
    weight_sem,
    token_sem,
    send_sem,
    recv_sem,
    factor_send,
    factor_recv,
    code_send,
    code_recv,
):
    n = depth_z * width_y * 2
    chunks = gathered.shape[0]
    rows_dev = gathered.shape[2]
    wide = gathered.shape[3]
    rows = n * rows_dev
    ff = weights.shape[2]
    rank = up_all.shape[2]
    me = lax.axis_index("owner")
    core = lax.rem(me, 2)
    y = lax.rem(me // 2, width_y)
    z = me // (2 * width_y)

    def index(zz, yy, cc):
        return (zz * width_y + yy) * 2 + cc

    def peer(j):
        return lax.rem(me + j, n)

    def token_copy(c):
        return pltpu.make_async_copy(
            tok_hbm.at[:, pl.ds(c * wide, wide)], gathered.at[c, me], token_sem.at[c]
        )

    for c in range(chunks):
        token_copy(c).start()
    up_copy = pltpu.make_async_copy(up_hbm.at[0], up_wide, local_sem.at[0])
    up_copy.start()

    def weight_copy(c):
        part = pl.ds(pl.multiple_of(c * wide, wide), wide)
        return pltpu.make_async_copy(w_hbm.at[:, part], weights.at[:, part], weight_sem.at[c])

    for c in range(chunks):
        weight_copy(c).start()
    down_copy = pltpu.make_async_copy(down_hbm.at[0], down, local_sem.at[1])
    down_copy.start()

    barrier = pltpu.get_barrier_semaphore()
    for j in range(1, n):
        pl.semaphore_signal(
            barrier, inc=1, device_id={"owner": peer(j)}, device_id_type=pl.DeviceIdType.MESH
        )
    pl.semaphore_wait(barrier, n - 1)

    def block_copy(kind, c, o, target):
        return pltpu.make_async_remote_copy(
            src_ref=gathered.at[c, o],
            dst_ref=gathered.at[c, o],
            send_sem=send_sem.at[kind, c, o],
            recv_sem=recv_sem.at[c, o],
            device_id={"owner": target},
            device_id_type=pl.DeviceIdType.MESH,
        )

    def upward(c, o):
        return block_copy(0, c, o, index(lax.rem(z + 1, depth_z), y, core))

    def downward(c, o):
        return block_copy(1, c, o, index(lax.rem(z + depth_z - 1, depth_z), y, core))

    def across(c, o):
        return block_copy(2, c, o, index(z, 1 - y, core))

    def sibling(c, o):
        return block_copy(3, c, o, index(z, y, 1 - core))

    def own_sends(c):
        token_copy(c).wait()

        @pl.when(z < depth_z - 1)
        def _():
            upward(c, me).start()

        @pl.when(z > 0)
        def _():
            downward(c, me).start()

        if width_y > 1:
            across(c, me).start()
        sibling(c, me).start()

    def factor_copy(j):
        return pltpu.make_async_remote_copy(
            src_ref=up_send.at[peer(j)],
            dst_ref=up_all.at[:, me],
            send_sem=factor_send.at[j],
            recv_sem=factor_recv.at[j],
            device_id={"owner": peer(j)},
            device_id_type=pl.DeviceIdType.MESH,
        )

    def code_copy(j):
        return pltpu.make_async_remote_copy(
            src_ref=packed.at[me],
            dst_ref=packed.at[me],
            send_sem=code_send.at[j],
            recv_sem=code_recv.at[j],
            device_id={"owner": peer(j)},
            device_id_type=pl.DeviceIdType.MESH,
        )

    for c in range(chunks):
        own_sends(c)
    up_copy.wait()
    for o in range(n):
        up_send[o] = up_wide[:, :, o * ff : (o + 1) * ff].astype(jnp.bfloat16)
    up_all[:, pl.ds(me, 1)] = up_send[pl.ds(me, 1)].reshape(2, 1, rank, ff)

    def hop(c, d):
        for side, arrive, last in ((-1, upward, depth_z - 1), (1, downward, 0)):

            @pl.when((z >= d) if side < 0 else (z + d < depth_z))
            def _():
                o = index(z + side * d, y, core)
                arrive(c, o).wait_recv()

                @pl.when(z != last)
                def _():
                    arrive(c, o).start()

                if width_y > 1:
                    across(c, o).start()
                sibling(c, o).start()

    def land(c, d):
        for zz, there in ((z - d, z >= d), (z + d, z + d < depth_z)):
            there = there if d > 0 else z >= 0

            @pl.when(there)
            def _():
                o = index(zz, 1 - y, core)
                across(c, o).wait_recv()
                sibling(c, o).start()

            if d == 0:
                break

    def complete(c):
        for zz in range(depth_z):
            for yy in range(width_y):
                sibling(c, index(zz, yy, 1 - core)).wait_recv()

    down_copy.wait()

    def code_dot(c):
        part = pl.ds(pl.multiple_of(c * wide, wide), wide)
        high, low = split_two(down[:, part])
        factors = jnp.concatenate([high] * 4 + [low] * 4, axis=0)
        value = lax.dot_general(
            gathered[c].reshape(rows, wide),
            factors,
            (((1,), (1,)), ((), ())),
            preferred_element_type=jnp.float32,
        )
        code_total[...] = value if c == 0 else code_total[...] + value

    def multiply(c):
        part = pl.ds(pl.multiple_of(c * wide, wide), wide)
        weight_copy(c).wait()
        for p in range(2):

            @pl.loop(0, ff // COLUMN_TILE)
            def _(t):
                columns = pl.ds(pl.multiple_of(t * COLUMN_TILE, COLUMN_TILE), COLUMN_TILE)
                value = jnp.dot(
                    gathered[c].reshape(rows, wide),
                    weights[p, part, columns],
                    preferred_element_type=jnp.float32,
                )
                total[p, :, columns] = value if c == 0 else total[p, :, columns] + value

    ids = id_ref[...]
    hit = ids == iota((rows, n), 1)
    home = jnp.sum(jnp.where(hit, owner_ref[...], 0).astype(jnp.float32), axis=1, keepdims=True)
    home = home.astype(jnp.int32)
    member = (home == iota((rows, 128), 1)).astype(jnp.float32)
    lower = (iota((rows, rows), 1) < iota((rows, rows), 0)).astype(jnp.bfloat16)
    before = jnp.dot(lower, member.astype(jnp.bfloat16), preferred_element_type=jnp.float32)
    slot = jnp.sum(before * member, axis=1, keepdims=True).astype(jnp.int32)
    slot_low, slot_high = lax.rem(slot, 8), slot // 8
    lane_group = iota((rows, 128), 1) // (2 * rank)
    pick = (slot_low == iota((rows, 8), 1)).astype(jnp.float32)
    back = (home * 8 + slot_low == iota((rows, n * 8), 1)).astype(jnp.float32)

    def share_codes():
        codes = code_total[:, :128] + code_total[:, 128:]
        placed = jnp.where((lane_group == slot_high) & (home == me), codes, 0.0)
        packed[me] = lax.dot_general(
            pick, placed, (((0,), (0,)), ((), ())), precision=HIGHEST, preferred_element_type=jnp.float32
        )
        for j in range(1, n):
            code_copy(j).start()

    def factors_of(tick):
        first = 1 + max(0, tick - FACTOR_TICK) * FACTORS_PER_TICK
        count = FACTORS_PER_TICK if tick >= FACTOR_TICK else 0
        return range(first, n if tick == chunks + depth_z - 1 else min(n, first + count))

    for tick in range(chunks + depth_z):
        for d in range(1, depth_z):
            if 0 <= tick - d + 1 < chunks:
                hop(tick - d + 1, d)
        if width_y > 1:
            for d in range(depth_z):
                if 0 <= tick - d < chunks:
                    land(tick - d, d)
        for j in factors_of(tick):
            factor_copy(j).start()
        if tick >= depth_z:
            complete(tick - depth_z)
            code_dot(tick - depth_z)
            if tick == chunks + depth_z - 1:
                share_codes()
            multiply(tick - depth_z)

    for j in range(1, n):
        code_copy(j).wait()
    rows_codes = jnp.dot(
        back, packed[...].reshape(n * 8, 128), precision=HIGHEST, preferred_element_type=jnp.float32
    )
    rows_codes = jnp.where(lane_group == slot_high, rows_codes, 0.0)
    spread = []
    for p in range(2):
        place = lax.rem(iota((128, n * rank), 0), 2 * rank)
        place = place == p * rank + lax.rem(iota((128, n * rank), 1), rank)
        value = jnp.dot(
            rows_codes, place.astype(jnp.float32), precision=HIGHEST, preferred_element_type=jnp.float32
        )
        spread.append(split_two(jnp.where(iota((rows, n * rank), 1) // rank == home, value, 0.0)))

    for j in range(1, n):
        factor_copy(j).wait()

    def preact(p, lo, hi):
        factors = up_all[p].reshape(n * rank, ff)[:, lo:hi]
        term = jnp.dot(spread[p][0], factors, preferred_element_type=jnp.float32)
        term += jnp.dot(spread[p][1], factors, preferred_element_type=jnp.float32)
        return total[p, :, lo:hi] + term.astype(jnp.bfloat16).astype(jnp.float32)

    for lo in range(0, ff, COLUMN_TILE):
        gate = preact(0, lo, lo + COLUMN_TILE)
        up = preact(1, lo, lo + COLUMN_TILE)
        out_ref[:, lo : lo + COLUMN_TILE] = (gate / (1.0 + jnp.exp(-gate)) * up).astype(out_ref.dtype)

    for c in range(chunks):
        for zz in range(depth_z):
            o = index(zz, y, core)

            @pl.when((z < depth_z - 1) & (zz <= z))
            def _():
                upward(c, o).wait_send()

            @pl.when((z > 0) & (zz >= z))
            def _():
                downward(c, o).wait_send()

            if width_y > 1:
                across(c, o).wait_send()
            for yy in range(width_y):
                sibling(c, index(zz, yy, core)).wait_send()


def fused(depth_z, width_y, tokens, base_weight, adapter_down, adapter_up, adapter_id, owner_of):
    n = depth_z * width_y * 2
    rows_dev, d = tokens.shape
    ff = base_weight.shape[2]
    rank = adapter_up.shape[2]
    rows = rows_dev * n
    wide = d // CHUNKS
    any_space = pl.BlockSpec(memory_space=pl.ANY)
    vmem = pl.BlockSpec(memory_space=pltpu.VMEM)
    dma = pltpu.SemaphoreType.DMA
    return pl.pallas_call(
        functools.partial(kernel, depth_z, width_y),
        out_shape=jax.ShapeDtypeStruct((rows, ff), jnp.bfloat16),
        in_specs=[vmem, vmem, any_space, any_space, any_space, any_space],
        out_specs=vmem,
        scratch_shapes=[
            pltpu.VMEM((CHUNKS, n, rows_dev, wide), jnp.bfloat16),
            pltpu.VMEM((2, d, ff), jnp.bfloat16),
            pltpu.VMEM((2 * rank, d), jnp.float32),
            pltpu.VMEM((2, rank, n * ff), jnp.float32),
            pltpu.VMEM((n, 2, rank, ff), jnp.bfloat16),
            pltpu.VMEM((2, n, rank, ff), jnp.bfloat16),
            pltpu.VMEM((n, 8, 128), jnp.float32),
            pltpu.VMEM((2, rows, ff), jnp.float32),
            pltpu.VMEM((rows, 256), jnp.float32),
            dma((2,)),
            dma((CHUNKS,)),
            dma((CHUNKS,)),
            dma((4, CHUNKS, n)),
            dma((CHUNKS, n)),
            dma((n,)),
            dma((n,)),
            dma((n,)),
            dma((n,)),
        ],
        compiler_params=pltpu.CompilerParams(
            collective_id=0, has_side_effects=True, vmem_limit_bytes=60 * 1024 * 1024
        ),
        cost_estimate=pl.CostEstimate(
            flops=4 * rows * d * ff, bytes_accessed=4 * d * ff, transcendentals=rows * ff
        ),
    )(adapter_id, owner_of.reshape(1, n), tokens, base_weight, adapter_down, adapter_up)


def solution(mesh):
    owners = mesh.shape["owner"]
    width_y = 4 // mesh.shape["groups"]
    depth_z = owners // (2 * width_y)
    plan = functools.partial(fused, depth_z, width_y) if owners <= 16 else on_device
    return jax.shard_map(
        plan,
        mesh=mesh,
        in_specs=(
            P(("groups", "owner"), None),
            P(None, None, "owner"),
            P(("groups", "owner"), None, None),
            P(("groups", "owner"), None, None, None),
            P("groups", None),
            P("groups"),
        ),
        out_specs=P("groups", "owner"),
        check_vma=False,
    )
```
